32 devices in a mesh: section: 2 (over core), fsdp: 4 (over y, x), replica: 4 (over z).
Axes of the slice: x: 2, y: 2, z: 4, core: 2. Of those that a mesh axis runs over, the one named last changes fastest.
Arguments:
- images: bfloat16 [64, 196, 512], P(('fsdp', 'replica')), may hold values from -6 to 6
- cotangent: bfloat16 [64, 196, 512], P(('fsdp', 'replica')), may hold values from -6 to 6
- ln1_gain: float32 [2, 512], P('section'), may hold values from 0.5 to 1.5
- ln1_bias: float32 [2, 512], P('section'), may hold values from -1.75 to 1.75
- qkv_weight: bfloat16 [2, 512, 1536], P('section', 'fsdp'), may hold values from -0.25 to 0.25
- qkv_bias: float32 [2, 1536], P('section'), may hold values from -1.75 to 1.75
- proj_weight: bfloat16 [2, 512, 512], P('section', 'fsdp'), may hold values from -1 to 1
- proj_bias: float32 [2, 512], P('section'), may hold values from -1.75 to 1.75
- ln2_gain: float32 [2, 512], P('section'), may hold values from 0.5 to 1.5
- ln2_bias: float32 [2, 512], P('section'), may hold values from -1.75 to 1.75
- fc1_weight: bfloat16 [2, 512, 2048], P('section', 'fsdp'), may hold values from -0.25 to 0.25
- fc1_bias: float32 [2, 2048], P('section'), may hold values from -1.75 to 1.75
- fc2_weight: bfloat16 [2, 2048, 512], P('section', 'fsdp'), may hold values from -0.1875 to 0.1875
- fc2_bias: float32 [2, 512], P('section'), may hold values from -1.75 to 1.75
- rel_table: float32 [2, 169, 16], P('section'), may hold values from -6 to 6
- rel_index: int32 [49, 49], replicated, may hold values from 0 to 168
- region: int32 [196], replicated, may hold values from 0 to 8, as said below
Outputs:
- activations: bfloat16 [2, 64, 196, 512], P('section', ('fsdp', 'replica'))
- input_grad: bfloat16 [2, 64, 196, 512], P('section', ('fsdp', 'replica'))
- grad_ln1_gain: float32 [2, 512], P('section')
- grad_ln1_bias: float32 [2, 512], P('section')
- grad_qkv_weight: float32 [2, 512, 1536], P('section', 'fsdp')
- grad_qkv_bias: float32 [2, 1536], P('section')
- grad_proj_weight: float32 [2, 512, 512], P('section', 'fsdp')
- grad_proj_bias: float32 [2, 512], P('section')
- grad_ln2_gain: float32 [2, 512], P('section')
- grad_ln2_bias: float32 [2, 512], P('section')
- grad_fc1_weight: float32 [2, 512, 2048], P('section', 'fsdp')
- grad_fc1_bias: float32 [2, 2048], P('section')
- grad_fc2_weight: float32 [2, 2048, 512], P('section', 'fsdp')
- grad_fc2_bias: float32 [2, 512], P('section')
- grad_rel_table: float32 [2, 169, 16], P('section')
The draws below stay inside these ranges and needn't reach their ends.
Inputs may be any that keep to these rules, and one draw needn't show every extreme that they name: `region`: labels of axis-aligned blocks, three bands of rows times three bands of columns, each band a run of positions.
All inputs are finite; a program needn't handle non-finite values.
Results may differ from the reference program's by a relative error of at most 0.019.
Values may be sent and summed in bfloat16 or wider, within the bound.
A program may use at most 192 MiB of HBM per device.

```python
import jax
import jax.numpy as jnp
from jax import lax

D = 512
HEADS = 16
HEAD_DIM = 32
FF = 2048
WIN = 7
SHIFT = 3
SIDE = 14
REL = 169
IMAGES = 64


def draw_region(key, part):
    key = jax.random.fold_in(key, 11)
    pieces = jax.random.split(key, 4)
    row_low = jax.random.randint(pieces[0], (), 4, 9)
    row_high = jax.random.randint(pieces[1], (), 10, SIDE)
    col_low = jax.random.randint(pieces[2], (), 4, 9)
    col_high = jax.random.randint(pieces[3], (), 10, SIDE)
    places = jnp.arange(SIDE, dtype=jnp.int32)
    rows = (places >= row_low).astype(jnp.int32) + (places >= row_high).astype(jnp.int32)
    cols = (places >= col_low).astype(jnp.int32) + (places >= col_high).astype(jnp.int32)
    return (rows[:, None] * 3 + cols[None, :]).reshape(SIDE * SIDE)


def plant(entries, rng, least, high):
    longest = entries.shape.index(max(entries.shape))
    spots = []
    for shift in (0, 1):
        where = [jax.random.randint(jax.random.fold_in(rng, axis), (), 0, length) for axis, length in enumerate(entries.shape)]
        where[longest] = (where[longest] + shift) % entries.shape[longest]
        spots.append(tuple(where))
    return entries.at[spots[0]].set(least).at[spots[1]].set(high)


def block_scale(key, dims, cuts, least, largest):
    factor_of = 1.0
    for dim, shards_of in cuts:
        draws = jax.random.uniform(jax.random.fold_in(jax.random.fold_in(key, 6), dim), (shards_of,), jnp.float32, least / len(cuts), largest / len(cuts))
        factor_of = factor_of * jnp.repeat(jnp.exp(draws), dims[dim] // shards_of).reshape((-1,) + (1,) * (len(dims) - 1 - dim))
    return factor_of


def scatter_about(key, dims, scale, reach, cuts=(), kind=jnp.bfloat16):
    level = block_scale(key, dims, cuts, -0.22, 0.18) if cuts else 1.0
    entries = jax.random.normal(key, dims, jnp.float32) * scale * level
    return jnp.minimum(jnp.maximum(entries, -reach), reach).astype(kind)


def setup_inputs(seed: int = 0) -> dict:
    key_list = jax.random.split(jax.random.key(seed), 18)
    return {
        "images": scatter_about(key_list[0], (IMAGES, SIDE * SIDE, D), 1.0, 6.0, ((0, 16),)),
        "cotangent": scatter_about(key_list[1], (IMAGES, SIDE * SIDE, D), 1.0, 6.0, ((0, 16),)),
        "ln1_gain": jnp.clip(1.0 + 0.1 * jax.random.normal(key_list[2], (2, D), jnp.float32), 0.5, 1.5),
        "ln1_bias": scatter_about(key_list[3], (2, D), 0.3, 1.75, ((0, 2),), jnp.float32),
        "qkv_weight": scatter_about(key_list[4], (2, D, 3 * D), D ** -0.5, 0.25, ((0, 2), (1, 4))),
        "qkv_bias": scatter_about(key_list[5], (2, 3 * D), 0.3, 1.75, ((0, 2),), jnp.float32),
        "proj_weight": scatter_about(key_list[6], (2, D, D), (D // 16) ** -0.5, 1.0, ((0, 2), (1, 4))),
        "proj_bias": scatter_about(key_list[7], (2, D), 0.3, 1.75, ((0, 2),), jnp.float32),
        "ln2_gain": jnp.clip(1.0 + 0.1 * jax.random.normal(key_list[8], (2, D), jnp.float32), 0.5, 1.5),
        "ln2_bias": scatter_about(key_list[9], (2, D), 0.3, 1.75, ((0, 2),), jnp.float32),
        "fc1_weight": scatter_about(key_list[10], (2, D, FF), D ** -0.5, 0.25, ((0, 2), (1, 4))),
        "fc1_bias": scatter_about(key_list[11], (2, FF), 0.3, 1.75, ((0, 2),), jnp.float32),
        "fc2_weight": scatter_about(key_list[12], (2, FF, D), (FF // 2) ** -0.5, 0.1875, ((0, 2), (1, 4))),
        "fc2_bias": scatter_about(key_list[13], (2, D), 0.3, 1.75, ((0, 2),), jnp.float32),
        "rel_table": scatter_about(key_list[14], (2, REL, HEADS), 1.0, 6.0, ((0, 2),), jnp.float32),
        "rel_index": plant(jax.random.randint(key_list[15], (WIN * WIN, WIN * WIN), 0, REL), jax.random.fold_in(key_list[15], 1), 0, REL - 1).astype(jnp.int32),
        "region": draw_region(jax.random.fold_in(key_list[17], 71), 0),
    }


@jax.custom_vjp
def low(v):
    return lax.optimization_barrier(v.astype(jnp.bfloat16)).astype(jnp.float32)

@jax.custom_vjp
def low_back(v):
    return v

def low_keep(v):
    return (low(v), None)

def low_pass(kept, grad):
    return (grad,)

def back_keep(v):
    return (v, None)

def back_low(kept, grad):
    return (low(grad),)
low.defvjp(low_keep, low_pass)
low_back.defvjp(back_keep, back_low)

def layer_norm(values, gain, offset):
    centre = values - lax.optimization_barrier(jnp.mean(values, -1, keepdims=True))
    spread = lax.optimization_barrier(jnp.mean(centre * centre, -1, keepdims=True))
    return centre * lax.rsqrt(spread + 1e-05) * gain + offset

def to_windows(field):
    count = field.shape[0]
    across = SIDE // WIN
    field = field.reshape(count, across, WIN, across, WIN, field.shape[-1])
    field = field.transpose(0, 1, 3, 2, 4, 5)
    return field.reshape(count * across * across, WIN * WIN, field.shape[-1])

def from_windows(blocks, count):
    across = SIDE // WIN
    blocks = blocks.reshape(count, across, across, WIN, WIN, blocks.shape[-1])
    blocks = blocks.transpose(0, 1, 3, 2, 4, 5)
    return blocks.reshape(count, SIDE, SIDE, blocks.shape[-1])

def layer(inputs, params, shifted, region, rel_index):
    gain_one, shift_one, w_qkv, bias_qkv, w_proj, bias_proj, gain_two, shift_two, w_fc1, bias_fc1, w_fc2, bias_fc2, table = params
    count = inputs.shape[0]
    normed = low(layer_norm(inputs, gain_one, shift_one))
    grid = normed.reshape(count, SIDE, SIDE, D)
    if shifted:
        grid = jnp.roll(grid, (-SHIFT, -SHIFT), (1, 2))
    windows = to_windows(grid)
    packed = low(low_back(jnp.matmul(windows, w_qkv, precision=lax.Precision.HIGHEST) + bias_qkv))
    heads = packed.reshape(-1, WIN * WIN, 3, HEADS, HEAD_DIM).transpose(2, 0, 3, 1, 4)
    scores = jnp.einsum('bhid,bhjd->bhij', heads[0], heads[1], precision=lax.Precision.HIGHEST) * HEAD_DIM ** (-0.5)
    scores = scores + table[rel_index].transpose(2, 0, 1)
    scores = scores.reshape(count, -1, HEADS, WIN * WIN, WIN * WIN)
    if shifted:
        labels = to_windows(region.reshape(1, SIDE, SIDE, 1))[:, :, 0]
        penalty = jnp.where(labels[:, :, None] != labels[:, None, :], -100.0, 0.0).astype(jnp.float32)
        scores = scores + penalty[None, :, None]
    scores = low_back(scores)
    probs = low(jax.nn.softmax(scores, -1)).reshape(-1, HEADS, WIN * WIN, WIN * WIN)
    mixed = jnp.einsum('bhij,bhjd->bihd', probs, heads[2], precision=lax.Precision.HIGHEST)
    attended = low(low_back(mixed.reshape(-1, WIN * WIN, D)))
    branch = low_back(jnp.matmul(attended, w_proj, precision=lax.Precision.HIGHEST) + bias_proj)
    branch = from_windows(branch, count)
    if shifted:
        branch = jnp.roll(branch, (SHIFT, SHIFT), (1, 2))
    middle = inputs + branch.reshape(count, SIDE * SIDE, D)
    normed_two = low(layer_norm(middle, gain_two, shift_two))
    hidden = low_back(jnp.matmul(normed_two, w_fc1, precision=lax.Precision.HIGHEST) + bias_fc1)
    activated = low(jax.nn.gelu(hidden, approximate=False))
    branch_two = low_back(jnp.matmul(activated, w_fc2, precision=lax.Precision.HIGHEST) + bias_fc2)
    return middle + branch_two

def reference(images, cotangent, ln1_gain, ln1_bias, qkv_weight, qkv_bias, proj_weight, proj_bias, ln2_gain, ln2_bias, fc1_weight, fc1_bias, fc2_weight, fc2_bias, rel_table, rel_index, region):
    every = (ln1_gain, ln1_bias, qkv_weight, qkv_bias, proj_weight, proj_bias, ln2_gain, ln2_bias, fc1_weight, fc1_bias, fc2_weight, fc2_bias, rel_table)
    params_zero = tuple((item[0].astype(jnp.float32) for item in every))
    params_one = tuple((item[1].astype(jnp.float32) for item in every))

    def first_layer(inputs, *params):
        return layer(inputs, params, False, region, rel_index)

    def second_layer(inputs, *params):
        return layer(inputs, params, True, region, rel_index)
    result_zero, pull_zero = jax.vjp(first_layer, images.astype(jnp.float32), *params_zero)
    sent = low(result_zero)
    result_one, pull_one = jax.vjp(second_layer, sent, *params_one)
    grads_one = pull_one(cotangent.astype(jnp.float32))
    passed = low(grads_one[0])
    grads_zero = pull_zero(passed)
    activations = jnp.stack([sent, result_one]).astype(jnp.bfloat16)
    input_grad = jnp.stack([grads_zero[0], passed]).astype(jnp.bfloat16)
    stacked = [jnp.stack([grads_zero[index + 1], grads_one[index + 1]]) for index in range(13)]
    return (activations, input_grad, stacked[0], stacked[1], stacked[2], stacked[3], stacked[4], stacked[5], stacked[6], stacked[7], stacked[8], stacked[9], stacked[10], stacked[11], stacked[12])
```

```python
import functools

import jax
import jax.numpy as jnp
import numpy as np
from jax import lax
from jax.experimental import pallas as pl
from jax.experimental.pallas import tpu as pltpu
from jax.sharding import PartitionSpec as P

D = 512
HEADS = 16
HEAD_DIM = 32
FF = 2048
WIN = 7
SHIFT = 3
SIDE = 14
REL = 169
TOKENS = SIDE * SIDE
SPOTS = WIN * WIN
PAD = 64
ACROSS = SIDE // WIN
WINDOWS = ACROSS * ACROSS
ROWS = WINDOWS * PAD
HALVES = 2
HALF_HEADS = HEADS // HALVES
HALF = HALF_HEADS * HEAD_DIM
WIDE = HALF_HEADS * PAD
SCALE = HEAD_DIM ** (-0.5)
FAR = -1e30
CHUNK = 512
VMEM = 56 * 2**20
F32 = jnp.float32
BF16 = jnp.bfloat16

NT = (((1,), (1,)), ((), ()))
TN = (((0,), (0,)), ((), ()))


def dot(left, right):
    return jnp.dot(left, right, preferred_element_type=F32)


def dot_nt(left, right):
    return lax.dot_general(left, right, NT, preferred_element_type=F32)


def dot_tn(left, right):
    return lax.dot_general(left, right, TN, preferred_element_type=F32)


def window_tokens(shift):
    tokens = np.full((ROWS,), -1, np.int32)
    for row in range(ROWS):
        window, spot = divmod(row, PAD)
        if spot < SPOTS:
            down = window // ACROSS * WIN + spot // WIN
            right = window % ACROSS * WIN + spot % WIN
            tokens[row] = (down + shift) % SIDE * SIDE + (right + shift) % SIDE
    return tokens


def placement(shift):
    return (window_tokens(shift)[:, None] == np.arange(TOKENS)[None, :]).astype(np.float32)


def head_mask():
    rows = lax.broadcasted_iota(jnp.int32, (WIDE, HALF), 0) // PAD
    columns = lax.broadcasted_iota(jnp.int32, (WIDE, HALF), 1) // HEAD_DIM
    return (rows == columns).astype(F32).astype(BF16)


def spread(block, mask):
    return jnp.concatenate([block] * HALF_HEADS, 0) * mask


def gather_heads(block, mask):
    kept = (block * mask.astype(F32)).reshape(HALF_HEADS, PAD, HALF)
    return jnp.sum(kept, 0)


def by_head(values, reduce, neutral):
    parts = []
    for start in range(0, values.shape[1], 2 * PAD):
        tile = values[:, start : start + 2 * PAD]
        low = lax.broadcasted_iota(jnp.int32, tile.shape, 1) < PAD
        early = reduce(jnp.where(low, tile, neutral), axis=1, keepdims=True)
        later = reduce(jnp.where(low, neutral, tile), axis=1, keepdims=True)
        parts.append(jnp.where(low, early, later))
    return jnp.concatenate(parts, 1)


def norm_stats(values):
    centre = values - jnp.mean(values, -1, keepdims=True)
    inverse = lax.rsqrt(jnp.mean(centre * centre, -1, keepdims=True) + 1e-05)
    return centre * inverse, inverse


def norm_back(grad, unit, inverse, gain):
    scaled = grad * gain
    inner = jnp.mean(scaled * unit, -1, keepdims=True)
    return inverse * (scaled - jnp.mean(scaled, -1, keepdims=True) - unit * inner)


def column_sum(values):
    return jnp.sum(values, 0, keepdims=True)


def attention_forward(
    x_ref, place_ref, wqkv_ref, wproj_ref, gain_ref, shift_ref, bqkv_ref, bproj_ref, bias_ref,
    normed_ref, packed_ref, probs_ref, attended_ref, middle_ref,
):
    count = x_ref.shape[0]
    for image in range(count):
        rows = pl.ds(image * ROWS, ROWS)
        field = dot(place_ref[...], x_ref[image])
        unit, _ = norm_stats(field)
        normed = (unit * gain_ref[...] + shift_ref[...]).astype(BF16)
        normed_ref[rows, :] = normed
        middle_ref[rows, :] = field
        packed_ref[rows, :] = (dot(normed, wqkv_ref[...]) + bqkv_ref[...]).astype(BF16)
    mask = head_mask()

    def window(index, carry):
        rows = pl.ds(pl.multiple_of(index * PAD, PAD), PAD)
        which = lax.rem(index, bias_ref.shape[0])
        for half in range(HALVES):
            columns = pl.ds(half * HALF, HALF)
            query = packed_ref[rows, columns]
            keys = spread(packed_ref[rows, pl.ds(D + half * HALF, HALF)], mask)
            values = spread(packed_ref[rows, pl.ds(2 * D + half * HALF, HALF)], mask)
            wide = pl.ds(half * WIDE, WIDE)
            scores = dot_nt(query, keys) * SCALE + bias_ref[which, :, wide]
            grown = jnp.exp(scores - by_head(scores, jnp.max, FAR))
            probs = grown / by_head(grown, jnp.sum, 0.0)
            probs_ref[rows, wide] = probs
            attended_ref[rows, columns] = dot(probs.astype(BF16), values).astype(BF16)
        return carry

    lax.fori_loop(0, count * WINDOWS, window, 0)
    for image in range(count):
        rows = pl.ds(image * ROWS, ROWS)
        middle_ref[rows, :] += dot(attended_ref[rows, :], wproj_ref[...]) + bproj_ref[...]


def feed_forward(
    middle_ref, back_ref, wfc1_ref, wfc2_ref, gain_ref, shift_ref, bfc1_ref, bfc2_ref,
    out_ref, normed_ref, activated_ref, slope_ref,
):
    for image in range(out_ref.shape[0]):
        rows = pl.ds(image * ROWS, ROWS)
        middle = middle_ref[rows, :]
        unit, _ = norm_stats(middle)
        normed = (unit * gain_ref[...] + shift_ref[...]).astype(BF16)
        normed_ref[rows, :] = normed
        for start in range(0, FF, CHUNK):
            columns = pl.ds(start, CHUNK)
            hidden = dot(normed, wfc1_ref[:, columns]) + bfc1_ref[:, columns]
            area = 0.5 * (1.0 + lax.erf(hidden * (0.5**0.5)))
            height = jnp.exp(-0.5 * hidden * hidden) * ((0.5 / np.pi) ** 0.5)
            activated_ref[rows, columns] = (hidden * area).astype(BF16)
            slope_ref[rows, columns] = (area + hidden * height).astype(BF16)
        result = middle + (dot(activated_ref[rows, :], wfc2_ref[...]) + bfc2_ref[...])
        out_ref[image] = dot(back_ref[...], result.astype(BF16)).astype(BF16)


def feed_backward(
    g_ref, place_ref, normed_ref, activated_ref, slope_ref, middle_ref, wfc1_ref, wfc2_ref, gain_ref,
    gfc1_ref, gfc2_ref, gmid_ref, gbfc1_ref, gbfc2_ref, ggain_ref, gshift_ref,
    gm_ref, gh_ref,
):
    count = g_ref.shape[0]
    gbfc1 = gbfc2 = ggain = gshift = 0.0
    for image in range(count):
        rows = pl.ds(image * ROWS, ROWS)
        incoming = dot(place_ref[...], g_ref[image])
        gm = incoming.astype(BF16)
        gm_ref[rows, :] = gm
        gbfc2 = gbfc2 + column_sum(incoming)
        sums = []
        for start in range(0, FF, CHUNK):
            columns = pl.ds(start, CHUNK)
            grad = dot_nt(gm, wfc2_ref[columns, :])
            gh = (grad * slope_ref[rows, columns].astype(F32)).astype(BF16)
            gh_ref[rows, columns] = gh
            sums.append(column_sum(gh.astype(F32)))
        gbfc1 = gbfc1 + jnp.concatenate(sums, 1)
        grad = dot_nt(gh_ref[rows, :], wfc1_ref[...])
        unit, inverse = norm_stats(middle_ref[rows, :])
        ggain = ggain + column_sum(grad * unit)
        gshift = gshift + column_sum(grad)
        gmid_ref[rows, :] = incoming + norm_back(grad, unit, inverse, gain_ref[...])
    gbfc1_ref[...] = gbfc1
    gbfc2_ref[...] = gbfc2
    ggain_ref[...] = ggain
    gshift_ref[...] = gshift
    for start in range(0, FF, CHUNK):
        columns = pl.ds(start, CHUNK)
        gfc2_ref[columns, :] = dot_tn(activated_ref[:, columns], gm_ref[...]).astype(BF16)
        gfc1_ref[:, columns] = dot_tn(normed_ref[...], gh_ref[:, columns]).astype(BF16)


def attention_backward(
    x_ref, place_ref, back_ref, gmid_ref, probs_ref, packed_ref, attended_ref, normed_ref,
    wqkv_ref, wproj_ref, gain_ref,
    gqkv_ref, gproj_ref, gin_ref, gbqkv_ref, gbproj_ref, ggain_ref, gshift_ref, gbias_ref,
    gb_ref, ga_ref, gpack_ref,
):
    count = x_ref.shape[0]
    gbproj = 0.0
    for image in range(count):
        rows = pl.ds(image * ROWS, ROWS)
        gb = gmid_ref[rows, :].astype(BF16)
        gb_ref[rows, :] = gb
        gbproj = gbproj + column_sum(gb.astype(F32))
        ga_ref[rows, :] = dot_nt(gb, wproj_ref[...]).astype(BF16)
    gbproj_ref[...] = gbproj
    gproj_ref[...] = dot_tn(attended_ref[...], gb_ref[...]).astype(BF16)
    mask = head_mask()
    gbias_ref[...] = jnp.zeros_like(gbias_ref)

    def window(index, carry):
        rows = pl.ds(pl.multiple_of(index * PAD, PAD), PAD)
        for half in range(HALVES):
            columns = pl.ds(half * HALF, HALF)
            key_columns = pl.ds(D + half * HALF, HALF)
            value_columns = pl.ds(2 * D + half * HALF, HALF)
            wide = pl.ds(half * WIDE, WIDE)
            query = packed_ref[rows, columns]
            keys = spread(packed_ref[rows, key_columns], mask)
            values = spread(packed_ref[rows, value_columns], mask)
            probs = probs_ref[rows, wide]
            ga = ga_ref[rows, columns]
            gp = dot_nt(ga, values)
            gs = (probs * (gp - by_head(gp * probs, jnp.sum, 0.0))).astype(BF16)
            gbias_ref[:, wide] += gs.astype(F32)
            gq = dot(gs, keys) * SCALE
            gk = gather_heads(dot_tn(gs, query), mask) * SCALE
            gv = gather_heads(dot_tn(probs.astype(BF16), ga), mask)
            gpack_ref[rows, columns] = gq.astype(BF16)
            gpack_ref[rows, key_columns] = gk.astype(BF16)
            gpack_ref[rows, value_columns] = gv.astype(BF16)
        return carry

    lax.fori_loop(0, count * WINDOWS, window, 0)
    gqkv_ref[...] = dot_tn(normed_ref[...], gpack_ref[...]).astype(BF16)
    gbqkv = ggain = gshift = 0.0
    for image in range(count):
        rows = pl.ds(image * ROWS, ROWS)
        gpack = gpack_ref[rows, :]
        gbqkv = gbqkv + column_sum(gpack.astype(F32))
        grad = dot_nt(gpack, wqkv_ref[...])
        unit, inverse = norm_stats(dot(place_ref[...], x_ref[image]))
        ggain = ggain + column_sum(grad * unit)
        gshift = gshift + column_sum(grad)
        gin = gmid_ref[rows, :] + norm_back(grad, unit, inverse, gain_ref[...])
        gin_ref[image] = dot(back_ref[...], gin.astype(BF16)).astype(BF16)
    gbqkv_ref[...] = gbqkv
    ggain_ref[...] = ggain
    gshift_ref[...] = gshift


def whole(array):
    return pl.BlockSpec(array.shape, lambda step, rank=len(array.shape): (0,) * rank)


def layer_of(array, layer):
    return pl.BlockSpec((array.shape[0] // 2,) + array.shape[1:], lambda step: (layer, 0))


def run(body, operands, outs, layer, weights, scratch=(), flops=0):
    outs = [jax.ShapeDtypeStruct(shape, kind) for shape, kind in outs]
    specs = [layer_of(item, layer) if index in weights else whole(item) for index, item in enumerate(operands)]
    return pl.pallas_call(
        body,
        grid=(1,),
        out_shape=outs,
        in_specs=specs,
        out_specs=[whole(item) for item in outs],
        scratch_shapes=list(scratch),
        cost_estimate=pl.CostEstimate(flops=flops, bytes_accessed=2**24, transcendentals=0),
        compiler_params=pltpu.CompilerParams(vmem_limit_bytes=VMEM),
    )(*operands)


def fetch_body(depth, *refs):
    count = (len(refs) - 5) // 2
    ins, outs = refs[:count], refs[count : 2 * count]
    far_send, far_recv, near_send, near_recv, local = refs[2 * count :]
    section, mine, replica = (lax.axis_index(name) for name in ("section", "fsdp", "replica"))
    sibling = (1 - section, mine, replica)
    peers = [(section, lax.rem(mine + step, depth), replica) for step in range(1, depth)]
    barrier = pltpu.get_barrier_semaphore()
    for device in peers + [sibling]:
        pl.semaphore_signal(barrier, inc=1, device_id=device, device_id_type=pl.DeviceIdType.MESH)
    pl.semaphore_wait(barrier, depth)

    def slot(item, owner):
        rows = ins[item].shape[0]
        start = pl.multiple_of((section * depth + owner) * rows, rows)
        return outs[item].at[pl.ds(start, rows)]

    def send(source, item, owner, device, leave, arrive):
        copy = pltpu.make_async_remote_copy(
            src_ref=source,
            dst_ref=slot(item, owner),
            send_sem=leave,
            recv_sem=arrive,
            device_id=device,
            device_id_type=pl.DeviceIdType.MESH,
        )
        copy.start()
        return copy

    far, near, kept = [], [], []
    for item in range(count):
        far.append([
            send(ins[item], item, mine, peers[step], far_send.at[item, step], far_recv.at[item, step])
            for step in range(depth - 1)
        ])
    for item in range(count):
        near.append(send(ins[item], item, mine, sibling, near_send.at[item, 0], near_recv.at[item, 0]))
        copy = pltpu.make_async_copy(ins[item], slot(item, mine), local.at[item])
        copy.start()
        kept.append(copy)
    for item in range(count):
        for step in range(1, depth):
            far[item][step - 1].wait_recv()
            owner = lax.rem(mine - step + depth, depth)
            near.append(
                send(slot(item, owner), item, owner, sibling, near_send.at[item, step], near_recv.at[item, step])
            )
    for item in range(count):
        for copy in far[item]:
            copy.wait_send()
        kept[item].wait()
    for copy in near:
        copy.wait()


def fetch(shards):
    depth = lax.axis_size("fsdp")
    count = len(shards)
    outs = [jax.ShapeDtypeStruct((2 * depth * item.shape[0], item.shape[1]), item.dtype) for item in shards]
    return pl.pallas_call(
        functools.partial(fetch_body, depth),
        out_shape=outs,
        in_specs=[pl.BlockSpec(memory_space=pl.ANY)] * count,
        out_specs=[pl.BlockSpec(memory_space=pl.ANY)] * count,
        scratch_shapes=[
            pltpu.SemaphoreType.DMA((count, depth - 1)),
            pltpu.SemaphoreType.DMA((count, depth - 1)),
            pltpu.SemaphoreType.DMA((count, depth)),
            pltpu.SemaphoreType.DMA((count, depth)),
            pltpu.SemaphoreType.DMA((count,)),
        ],
        compiler_params=pltpu.CompilerParams(collective_id=1, has_side_effects=True),
    )(*shards)


def pick(first, early, later):
    return jnp.where(first, early, later)


def on_device(
    images, cotangent, ln1_gain, ln1_bias, qkv_weight, qkv_bias, proj_weight, proj_bias, ln2_gain, ln2_bias,
    fc1_weight, fc1_bias, fc2_weight, fc2_bias, rel_table, rel_index, region,
):
    section = lax.axis_index("section")
    first = section == 0
    halves = lax.axis_size("section")
    count = images.shape[0] // halves
    every = ("section", "fsdp", "replica")
    swap = [(0, 1), (1, 0)]

    small = (ln1_gain, ln1_bias, qkv_bias, proj_bias, ln2_gain, ln2_bias, fc1_bias, fc2_bias, rel_table)
    sizes = [item[0].size for item in small]
    flat = jnp.concatenate([item.reshape(1, -1) for item in small], 1)
    both = lax.all_gather(flat, "section", axis=0, tiled=True)
    params = []
    for layer in range(2):
        pieces, start = [], 0
        for size in sizes:
            pieces.append(both[layer : layer + 1, start : start + size])
            start += size
        params.append(pieces)

    w_qkv, w_proj, w_fc1, w_fc2 = fetch([item[0] for item in (qkv_weight, proj_weight, fc1_weight, fc2_weight)])

    mine_x = lax.dynamic_slice_in_dim(images, section * count, count, 0)
    mine_g = lax.dynamic_slice_in_dim(cotangent, section * count, count, 0)

    edge = PAD - SPOTS
    index = jnp.pad(rel_index, ((0, edge), (0, edge)), constant_values=-1)
    onehot = (index.reshape(-1, 1) == jnp.arange(REL, dtype=jnp.int32)[None, :]).astype(F32)
    tables = jnp.concatenate([params[layer][8].reshape(REL, HEADS) for layer in range(2)], 1)
    spots = jnp.dot(onehot, tables, precision=lax.Precision.HIGHEST)
    spots = spots.reshape(PAD, PAD, 2, HEADS).transpose(2, 0, 3, 1)
    absent = jnp.where(jnp.arange(PAD) < SPOTS, 0.0, FAR).astype(F32)
    spots = spots + absent
    labels = region[np.maximum(window_tokens(0), 0)].reshape(WINDOWS, PAD)
    penalty = jnp.where(labels[:, :, None] != labels[:, None, :], -100.0, 0.0).astype(F32)
    biases = [
        spots[0].reshape(1, PAD, HEADS * PAD),
        (spots[1][None] + penalty[:, :, None, :]).reshape(WINDOWS, PAD, HEADS * PAD),
    ]

    places = [jnp.asarray(placement(shift), BF16) for shift in (0, SHIFT)]
    backs = [jnp.asarray(placement(shift).T, BF16) for shift in (0, SHIFT)]
    rows = count * ROWS
    dense = 2 * rows * D * D

    def forward(x, layer):
        gain_one, shift_one, b_qkv, b_proj, gain_two, shift_two, b_fc1, b_fc2, _ = params[layer]
        normed, packed, probs, attended, middle = run(
            attention_forward,
            (x, places[layer], w_qkv, w_proj, gain_one, shift_one, b_qkv, b_proj, biases[layer]),
            [((rows, D), BF16), ((rows, 3 * D), BF16), ((rows, HEADS * PAD), F32), ((rows, D), BF16), ((rows, D), F32)],
            layer, (2, 3), flops=12 * dense,
        )
        out, normed_two, activated, slope = run(
            feed_forward,
            (middle, backs[layer], w_fc1, w_fc2, gain_two, shift_two, b_fc1, b_fc2),
            [((count, TOKENS, D), BF16), ((rows, D), BF16), ((rows, FF), BF16), ((rows, FF), BF16)],
            layer, (2, 3), flops=12 * dense,
        )
        return out, (x, normed, packed, probs, attended, middle, normed_two, activated, slope)

    def backward(g, kept, layer):
        x, normed, packed, probs, attended, middle, normed_two, activated, slope = kept
        gain_one, gain_two = params[layer][0], params[layer][4]
        row = lambda width: ((1, width), F32)
        gfc1, gfc2, gmid, gbfc1, gbfc2, ggain2, gshift2 = run(
            feed_backward,
            (g, places[layer], normed_two, activated, slope, middle, w_fc1, w_fc2, gain_two),
            [((D, FF), BF16), ((FF, D), BF16), ((rows, D), F32), row(FF), row(D), row(D), row(D)],
            layer, (6, 7),
            (pltpu.VMEM((rows, D), BF16), pltpu.VMEM((rows, FF), BF16)), flops=20 * dense,
        )
        gqkv, gproj, gin, gbqkv, gbproj, ggain1, gshift1, gbias = run(
            attention_backward,
            (x, places[layer], backs[layer], gmid, probs, packed, attended, normed, w_qkv, w_proj, gain_one),
            [((D, 3 * D), BF16), ((D, D), BF16), ((count, TOKENS, D), BF16), row(3 * D), row(D), row(D), row(D),
             ((PAD, HEADS * PAD), F32)],
            layer, (8, 9),
            (pltpu.VMEM((rows, D), BF16), pltpu.VMEM((rows, D), BF16), pltpu.VMEM((rows, 3 * D), BF16)),
            flops=30 * dense,
        )
        gbias = gbias.reshape(PAD, HEADS, PAD).transpose(0, 2, 1).reshape(PAD * PAD, HEADS)
        gtable = jnp.dot(onehot.T, gbias, precision=lax.Precision.HIGHEST)
        minor = (ggain1, gshift1, gbqkv, gbproj, ggain2, gshift2, gbfc1, gbfc2, gtable.reshape(1, -1))
        minor = lax.psum(jnp.concatenate(minor, 1), every)
        owned = [reduce_rows(item) for item in (gfc2, gfc1, gproj, gqkv)]
        return gin, owned[::-1], minor

    def reduce_rows(grad):
        part = lax.psum_scatter(grad, ("fsdp", "section"), scatter_dimension=0, tiled=True)
        part = lax.psum_scatter(part, "replica", scatter_dimension=0, tiled=True)
        return lax.all_gather(part, "replica", axis=0, tiled=True)

    def exchange(early, later):
        other = lax.ppermute(pick(first, later, early), "section", swap)
        own = pick(first, early, later)
        return jnp.concatenate([pick(first, own, other), pick(first, other, own)], 0)

    act_zero, kept_zero = forward(mine_x, 0)
    act_one, kept_one = forward(act_zero, 1)
    gin_one, owned_one, minor_one = backward(mine_g, kept_one, 1)
    gin_zero, owned_zero, minor_zero = backward(gin_one, kept_zero, 0)
    activations = exchange(act_zero, act_one)
    input_grad = exchange(gin_zero, gin_one)
    owned = [exchange(early, later).astype(F32)[None] for early, later in zip(owned_zero, owned_one)]
    minor = pick(first, minor_zero, minor_one)
    minors, start = [], 0
    for size, item in zip(sizes, small):
        minors.append(minor[:, start : start + size].reshape(item.shape))
        start += size
    return (
        activations[None], input_grad[None],
        minors[0], minors[1], owned[0], minors[2], owned[1], minors[3], minors[4], minors[5],
        owned[2], minors[6], owned[3], minors[7], minors[8],
    )


def solution(mesh):
    sliced = P("section", "fsdp", None)
    vector = P("section", None)
    tokens = P(("fsdp", "replica"), None, None)
    in_specs = (
        tokens, tokens, vector, vector, sliced, vector, sliced, vector, vector, vector,
        sliced, vector, sliced, vector, P("section", None, None), P(), P(),
    )
    result = P("section", ("fsdp", "replica"), None, None)
    out_specs = (
        result, result, vector, vector, sliced, vector, sliced, vector, vector, vector,
        sliced, vector, sliced, vector, P("section", None, None),
    )
    return jax.shard_map(on_device, mesh=mesh, in_specs=in_specs, out_specs=out_specs, check_vma=False)
```

```python
import functools

import jax
import jax.numpy as jnp
import numpy as np
from jax import lax
from jax.experimental import pallas as pl
from jax.experimental.pallas import tpu as pltpu
from jax.sharding import PartitionSpec as P

D = 512
HEADS = 16
HEAD_DIM = 32
FF = 2048
WIN = 7
SHIFT = 3
SIDE = 14
REL = 169
TOKENS = SIDE * SIDE
SPOTS = WIN * WIN
PAD = 64
ACROSS = SIDE // WIN
WINDOWS = ACROSS * ACROSS
ROWS = WINDOWS * PAD
HALVES = 2
HALF_HEADS = HEADS // HALVES
HALF = HALF_HEADS * HEAD_DIM
WIDE = HALF_HEADS * PAD
SCALE = HEAD_DIM ** (-0.5)
FAR = -1e30
CHUNK = 512
BLOCK = 32
VMEM = 56 * 2**20
F32 = jnp.float32
BF16 = jnp.bfloat16

NT = (((1,), (1,)), ((), ()))
TN = (((0,), (0,)), ((), ()))


def dot(left, right):
    return jnp.dot(left, right, preferred_element_type=F32)


def dot_nt(left, right):
    return lax.dot_general(left, right, NT, preferred_element_type=F32)


def dot_tn(left, right):
    return lax.dot_general(left, right, TN, preferred_element_type=F32)


def window_tokens(shift):
    tokens = np.full((ROWS,), -1, np.int32)
    for row in range(ROWS):
        window, spot = divmod(row, PAD)
        if spot < SPOTS:
            down = window // ACROSS * WIN + spot // WIN
            right = window % ACROSS * WIN + spot % WIN
            tokens[row] = (down + shift) % SIDE * SIDE + (right + shift) % SIDE
    return tokens


def placement(shift):
    return (window_tokens(shift)[:, None] == np.arange(TOKENS)[None, :]).astype(np.float32)


def head_mask():
    rows = lax.broadcasted_iota(jnp.int32, (WIDE, HALF), 0) // PAD
    columns = lax.broadcasted_iota(jnp.int32, (WIDE, HALF), 1) // HEAD_DIM
    return (rows == columns).astype(F32).astype(BF16)


def spread(block, mask):
    return jnp.concatenate([block] * HALF_HEADS, 0) * mask


def gather_heads(block, mask):
    kept = (block * mask.astype(F32)).reshape(HALF_HEADS, PAD, HALF)
    return jnp.sum(kept, 0)


def by_head(values, reduce, neutral):
    parts = []
    for start in range(0, values.shape[1], 2 * PAD):
        tile = values[:, start : start + 2 * PAD]
        low = lax.broadcasted_iota(jnp.int32, tile.shape, 1) < PAD
        early = reduce(jnp.where(low, tile, neutral), axis=1, keepdims=True)
        later = reduce(jnp.where(low, neutral, tile), axis=1, keepdims=True)
        parts.append(jnp.where(low, early, later))
    return jnp.concatenate(parts, 1)


def norm_stats(values):
    centre = values - jnp.mean(values, -1, keepdims=True)
    inverse = lax.rsqrt(jnp.mean(centre * centre, -1, keepdims=True) + 1e-05)
    return centre * inverse, inverse


def norm_back(grad, unit, inverse, gain):
    scaled = grad * gain
    inner = jnp.mean(scaled * unit, -1, keepdims=True)
    return inverse * (scaled - jnp.mean(scaled, -1, keepdims=True) - unit * inner)


def column_sum(values):
    return jnp.sum(values, 0, keepdims=True)


def attention_forward(
    x_ref, place_ref, wqkv_ref, wproj_ref, gain_ref, shift_ref, bqkv_ref, bproj_ref, bias_ref,
    normed_ref, packed_ref, probs_ref, attended_ref, middle_ref,
):
    count = x_ref.shape[0]
    for image in range(count):
        rows = pl.ds(image * ROWS, ROWS)
        field = dot(place_ref[...], x_ref[image])
        unit, _ = norm_stats(field)
        normed = (unit * gain_ref[...] + shift_ref[...]).astype(BF16)
        normed_ref[rows, :] = normed
        middle_ref[rows, :] = field
        packed_ref[rows, :] = (dot(normed, wqkv_ref[...]) + bqkv_ref[...]).astype(BF16)
    mask = head_mask()

    def window(index, carry):
        rows = pl.ds(pl.multiple_of(index * PAD, PAD), PAD)
        which = lax.rem(index, bias_ref.shape[0])
        for half in range(HALVES):
            columns = pl.ds(half * HALF, HALF)
            query = packed_ref[rows, columns]
            keys = spread(packed_ref[rows, pl.ds(D + half * HALF, HALF)], mask)
            values = spread(packed_ref[rows, pl.ds(2 * D + half * HALF, HALF)], mask)
            wide = pl.ds(half * WIDE, WIDE)
            scores = dot_nt(query, keys) * SCALE + bias_ref[which, :, wide]
            grown = jnp.exp(scores - by_head(scores, jnp.max, FAR))
            probs = grown / by_head(grown, jnp.sum, 0.0)
            probs_ref[rows, wide] = probs
            attended_ref[rows, columns] = dot(probs.astype(BF16), values).astype(BF16)
        return carry

    lax.fori_loop(0, count * WINDOWS, window, 0)
    for image in range(count):
        rows = pl.ds(image * ROWS, ROWS)
        middle_ref[rows, :] += dot(attended_ref[rows, :], wproj_ref[...]) + bproj_ref[...]


def feed_forward(
    middle_ref, back_ref, wfc1_ref, wfc2_ref, gain_ref, shift_ref, bfc1_ref, bfc2_ref,
    out_ref, normed_ref, activated_ref, slope_ref,
):
    for image in range(out_ref.shape[0]):
        rows = pl.ds(image * ROWS, ROWS)
        middle = middle_ref[rows, :]
        unit, _ = norm_stats(middle)
        normed = (unit * gain_ref[...] + shift_ref[...]).astype(BF16)
        normed_ref[rows, :] = normed
        for start in range(0, FF, CHUNK):
            columns = pl.ds(start, CHUNK)
            hidden = dot(normed, wfc1_ref[:, columns]) + bfc1_ref[:, columns]
            area = 0.5 * (1.0 + lax.erf(hidden * (0.5**0.5)))
            height = jnp.exp(-0.5 * hidden * hidden) * ((0.5 / np.pi) ** 0.5)
            activated_ref[rows, columns] = (hidden * area).astype(BF16)
            slope_ref[rows, columns] = (area + hidden * height).astype(BF16)
        result = middle + (dot(activated_ref[rows, :], wfc2_ref[...]) + bfc2_ref[...])
        out_ref[image] = dot(back_ref[...], result.astype(BF16)).astype(BF16)


def feed_backward(
    g_ref, place_ref, normed_ref, activated_ref, slope_ref, middle_ref, wfc1_ref, wfc2_ref, gain_ref,
    gfc1_ref, gfc2_ref, gmid_ref, gbfc1_ref, gbfc2_ref, ggain_ref, gshift_ref,
    gm_ref, gh_ref,
):
    count = g_ref.shape[0]
    gbfc1 = gbfc2 = ggain = gshift = 0.0
    for image in range(count):
        rows = pl.ds(image * ROWS, ROWS)
        incoming = dot(place_ref[...], g_ref[image])
        gm = incoming.astype(BF16)
        gm_ref[rows, :] = gm
        gbfc2 = gbfc2 + column_sum(incoming)
        sums = []
        for start in range(0, FF, CHUNK):
            columns = pl.ds(start, CHUNK)
            grad = dot_nt(gm, wfc2_ref[columns, :])
            gh = (grad * slope_ref[rows, columns].astype(F32)).astype(BF16)
            gh_ref[rows, columns] = gh
            sums.append(column_sum(gh.astype(F32)))
        gbfc1 = gbfc1 + jnp.concatenate(sums, 1)
        grad = dot_nt(gh_ref[rows, :], wfc1_ref[...])
        unit, inverse = norm_stats(middle_ref[rows, :])
        ggain = ggain + column_sum(grad * unit)
        gshift = gshift + column_sum(grad)
        gmid_ref[rows, :] = incoming + norm_back(grad, unit, inverse, gain_ref[...])
    gbfc1_ref[...] = gbfc1
    gbfc2_ref[...] = gbfc2
    ggain_ref[...] = ggain
    gshift_ref[...] = gshift
    for start in range(0, FF, CHUNK):
        columns = pl.ds(start, CHUNK)
        gfc2_ref[columns, :] = dot_tn(activated_ref[:, columns], gm_ref[...]).astype(BF16)
        gfc1_ref[:, columns] = dot_tn(normed_ref[...], gh_ref[:, columns]).astype(BF16)


def attention_backward(
    x_ref, place_ref, back_ref, gmid_ref, probs_ref, packed_ref, attended_ref, normed_ref,
    wqkv_ref, wproj_ref, gain_ref,
    gqkv_ref, gproj_ref, gin_ref, gbqkv_ref, gbproj_ref, ggain_ref, gshift_ref, gbias_ref,
    gb_ref, ga_ref, gpack_ref,
):
    count = x_ref.shape[0]
    gbproj = 0.0
    for image in range(count):
        rows = pl.ds(image * ROWS, ROWS)
        gb = gmid_ref[rows, :].astype(BF16)
        gb_ref[rows, :] = gb
        gbproj = gbproj + column_sum(gb.astype(F32))
        ga_ref[rows, :] = dot_nt(gb, wproj_ref[...]).astype(BF16)
    gbproj_ref[...] = gbproj
    gproj_ref[...] = dot_tn(attended_ref[...], gb_ref[...]).astype(BF16)
    mask = head_mask()
    gbias_ref[...] = jnp.zeros_like(gbias_ref)

    def window(index, carry):
        rows = pl.ds(pl.multiple_of(index * PAD, PAD), PAD)
        for half in range(HALVES):
            columns = pl.ds(half * HALF, HALF)
            key_columns = pl.ds(D + half * HALF, HALF)
            value_columns = pl.ds(2 * D + half * HALF, HALF)
            wide = pl.ds(half * WIDE, WIDE)
            query = packed_ref[rows, columns]
            keys = spread(packed_ref[rows, key_columns], mask)
            values = spread(packed_ref[rows, value_columns], mask)
            probs = probs_ref[rows, wide]
            ga = ga_ref[rows, columns]
            gp = dot_nt(ga, values)
            gs = (probs * (gp - by_head(gp * probs, jnp.sum, 0.0))).astype(BF16)
            gbias_ref[:, wide] += gs.astype(F32)
            gq = dot(gs, keys) * SCALE
            gk = gather_heads(dot_tn(gs, query), mask) * SCALE
            gv = gather_heads(dot_tn(probs.astype(BF16), ga), mask)
            gpack_ref[rows, columns] = gq.astype(BF16)
            gpack_ref[rows, key_columns] = gk.astype(BF16)
            gpack_ref[rows, value_columns] = gv.astype(BF16)
        return carry

    lax.fori_loop(0, count * WINDOWS, window, 0)
    gqkv_ref[...] = dot_tn(normed_ref[...], gpack_ref[...]).astype(BF16)
    gbqkv = ggain = gshift = 0.0
    for image in range(count):
        rows = pl.ds(image * ROWS, ROWS)
        gpack = gpack_ref[rows, :]
        gbqkv = gbqkv + column_sum(gpack.astype(F32))
        grad = dot_nt(gpack, wqkv_ref[...])
        unit, inverse = norm_stats(dot(place_ref[...], x_ref[image]))
        ggain = ggain + column_sum(grad * unit)
        gshift = gshift + column_sum(grad)
        gin = gmid_ref[rows, :] + norm_back(grad, unit, inverse, gain_ref[...])
        gin_ref[image] = dot(back_ref[...], gin.astype(BF16)).astype(BF16)
    gbqkv_ref[...] = gbqkv
    ggain_ref[...] = ggain
    gshift_ref[...] = gshift


def whole(array):
    return pl.BlockSpec(array.shape, lambda step, rank=len(array.shape): (0,) * rank)


def layer_of(array, layer):
    return pl.BlockSpec((array.shape[0] // 2,) + array.shape[1:], lambda step: (layer, 0))


def run(body, operands, outs, layer, weights, scratch=(), flops=0):
    outs = [jax.ShapeDtypeStruct(shape, kind) for shape, kind in outs]
    specs = [layer_of(item, layer) if index in weights else whole(item) for index, item in enumerate(operands)]
    return pl.pallas_call(
        body,
        grid=(1,),
        out_shape=outs,
        in_specs=specs,
        out_specs=[whole(item) for item in outs],
        scratch_shapes=list(scratch),
        cost_estimate=pl.CostEstimate(flops=flops, bytes_accessed=2**24, transcendentals=0),
        compiler_params=pltpu.CompilerParams(vmem_limit_bytes=VMEM),
    )(*operands)


def fetch_body(depth, *refs):
    count = (len(refs) - 5) // 2
    ins, outs = refs[:count], refs[count : 2 * count]
    far_send, far_recv, near_send, near_recv, local = refs[2 * count :]
    section, mine, replica = (lax.axis_index(name) for name in ("section", "fsdp", "replica"))
    sibling = (1 - section, mine, replica)
    peers = [(section, lax.rem(mine + step, depth), replica) for step in range(1, depth)]
    barrier = pltpu.get_barrier_semaphore()
    for device in peers + [sibling]:
        pl.semaphore_signal(barrier, inc=1, device_id=device, device_id_type=pl.DeviceIdType.MESH)
    pl.semaphore_wait(barrier, depth)

    def slot(item, owner):
        rows = ins[item].shape[0]
        start = pl.multiple_of((section * depth + owner) * rows, rows)
        return outs[item].at[pl.ds(start, rows)]

    def send(source, item, owner, device, leave, arrive):
        copy = pltpu.make_async_remote_copy(
            src_ref=source,
            dst_ref=slot(item, owner),
            send_sem=leave,
            recv_sem=arrive,
            device_id=device,
            device_id_type=pl.DeviceIdType.MESH,
        )
        copy.start()
        return copy

    far, near, kept = [], [], []
    for item in range(count):
        far.append([
            send(ins[item], item, mine, peers[step], far_send.at[item, step], far_recv.at[item, step])
            for step in range(depth - 1)
        ])
    for item in range(count):
        near.append(send(ins[item], item, mine, sibling, near_send.at[item, 0], near_recv.at[item, 0]))
        copy = pltpu.make_async_copy(ins[item], slot(item, mine), local.at[item])
        copy.start()
        kept.append(copy)
    for item in range(count):
        for step in range(1, depth):
            far[item][step - 1].wait_recv()
            owner = lax.rem(mine - step + depth, depth)
            near.append(
                send(slot(item, owner), item, owner, sibling, near_send.at[item, step], near_recv.at[item, step])
            )
    for item in range(count):
        for copy in far[item]:
            copy.wait_send()
        kept[item].wait()
    for copy in near:
        copy.wait()


def fetch(shards):
    depth = lax.axis_size("fsdp")
    count = len(shards)
    outs = [jax.ShapeDtypeStruct((2 * depth * item.shape[0], item.shape[1]), item.dtype) for item in shards]
    return pl.pallas_call(
        functools.partial(fetch_body, depth),
        out_shape=outs,
        in_specs=[pl.BlockSpec(memory_space=pl.ANY)] * count,
        out_specs=[pl.BlockSpec(memory_space=pl.ANY)] * count,
        scratch_shapes=[
            pltpu.SemaphoreType.DMA((count, depth - 1)),
            pltpu.SemaphoreType.DMA((count, depth - 1)),
            pltpu.SemaphoreType.DMA((count, depth)),
            pltpu.SemaphoreType.DMA((count, depth)),
            pltpu.SemaphoreType.DMA((count,)),
        ],
        compiler_params=pltpu.CompilerParams(collective_id=1, has_side_effects=True),
    )(*shards)


def reduce_body(depth, chain, *refs):
    units = 4
    early, later, outs = refs[:units], refs[units : 2 * units], refs[2 * units : 3 * units]
    near, held, peer, sums, outer_in, inner_in = [
        refs[(3 + step) * units : (4 + step) * units] for step in range(6)
    ]
    near_send, near_recv, far_send, far_recv, in_send, out_send, outer_recv, inner_recv = refs[9 * units :]
    section, mine, replica = (lax.axis_index(name) for name in ("section", "fsdp", "replica"))
    sibling = (1 - section, mine, replica)
    peers = [(section, lax.rem(mine + step, depth), replica) for step in range(1, depth)]
    half = chain // 2
    toward = jnp.where(replica < half, 1, -1)
    inner = (section, mine, replica + toward)
    outer = (section, mine, replica - toward)
    has_outer = jnp.logical_and(replica != 0, replica != chain - 1)
    central = jnp.logical_or(replica == half - 1, replica == half)
    mesh_ids = pl.DeviceIdType.MESH

    barrier = pltpu.get_barrier_semaphore()
    for device in peers + [sibling, inner]:
        pl.semaphore_signal(barrier, inc=1, device_id=device, device_id_type=mesh_ids)

    @pl.when(has_outer)
    def _():
        pl.semaphore_signal(barrier, inc=1, device_id=outer, device_id_type=mesh_ids)

    @pl.when(has_outer)
    def _():
        pl.semaphore_wait(barrier, depth + 2)

    @pl.when(jnp.logical_not(has_outer))
    def _():
        pl.semaphore_wait(barrier, depth + 1)

    def remote(source, target, leave, arrive, device):
        return pltpu.make_async_remote_copy(
            src_ref=source, dst_ref=target, send_sem=leave, recv_sem=arrive,
            device_id=device, device_id_type=mesh_ids,
        )

    def blocks(rows, body):
        def step(index, carry):
            body(pl.multiple_of(index * BLOCK, BLOCK))
            return carry

        lax.fori_loop(0, rows // BLOCK, step, 0)

    def near_copy(unit, source):
        return remote(source, near[unit], near_send.at[unit], near_recv.at[unit], sibling)

    def far_copy(unit, step):
        rows = sums[unit].shape[0]
        owner = lax.rem(mine + step, depth)
        source = held[unit].at[pl.ds(pl.multiple_of(owner * rows, rows), rows)]
        target = peer[unit].at[pl.ds((step - 1) * rows, rows)]
        return remote(source, target, far_send.at[unit, step - 1], far_recv.at[unit, step - 1], peers[step - 1])

    def send_inner(unit):
        @pl.when(central)
        def _():
            remote(sums[unit], inner_in[unit], in_send.at[unit], inner_recv.at[unit], inner).start()

        @pl.when(jnp.logical_not(central))
        def _():
            remote(sums[unit], outer_in[unit], in_send.at[unit], outer_recv.at[unit], inner).start()

    for unit in range(units):
        @pl.when(section == 0)
        def _():
            near_copy(unit, later[unit]).start()

        @pl.when(section != 0)
        def _():
            near_copy(unit, early[unit]).start()

    for unit in range(units):
        near_copy(unit, early[unit]).wait_recv()

        def combine(own):
            def add(start):
                rows = pl.ds(start, BLOCK)
                total = own[unit][rows, :].astype(F32) + near[unit][rows, :].astype(F32)
                held[unit][rows, :] = total.astype(BF16)

            blocks(own[unit].shape[0], add)

        @pl.when(section == 0)
        def _():
            combine(early)

        @pl.when(section != 0)
        def _():
            combine(later)

        for step in range(1, depth):
            far_copy(unit, step).start()

    def gather_peers(unit):
        rows = sums[unit].shape[0]
        for step in range(1, depth):
            far_copy(unit, step).wait_recv()

        def add(start):
            total = held[unit][pl.ds(pl.multiple_of(mine * rows + start, BLOCK), BLOCK), :].astype(F32)
            for step in range(1, depth):
                total = total + peer[unit][pl.ds((step - 1) * rows + start, BLOCK), :].astype(F32)
            sums[unit][pl.ds(start, BLOCK), :] = total.astype(BF16)

        blocks(rows, add)

        @pl.when(jnp.logical_not(has_outer))
        def _():
            send_inner(unit)

    def inward(unit):
        @pl.when(has_outer)
        def _():
            remote(sums[unit], outer_in[unit], in_send.at[unit], outer_recv.at[unit], inner).wait_recv()

            def add(start):
                rows = pl.ds(start, BLOCK)
                total = sums[unit][rows, :].astype(F32) + outer_in[unit][rows, :].astype(F32)
                sums[unit][rows, :] = total.astype(BF16)

            blocks(sums[unit].shape[0], add)
            send_inner(unit)

    def outward(unit):
        remote(sums[unit], inner_in[unit], in_send.at[unit], inner_recv.at[unit], inner).wait()

        @pl.when(central)
        def _():
            def add(start):
                rows = pl.ds(start, BLOCK)
                total = sums[unit][rows, :].astype(F32) + inner_in[unit][rows, :].astype(F32)
                sums[unit][rows, :] = total.astype(BF16)

            blocks(sums[unit].shape[0], add)

        @pl.when(jnp.logical_not(central))
        def _():
            def move(start):
                rows = pl.ds(start, BLOCK)
                sums[unit][rows, :] = inner_in[unit][rows, :]

            blocks(sums[unit].shape[0], move)

        @pl.when(has_outer)
        def _():
            remote(sums[unit], inner_in[unit], out_send.at[unit], inner_recv.at[unit], outer).start()

        def widen(start):
            rows = pl.ds(start, BLOCK)
            outs[unit][rows, :] = sums[unit][rows, :].astype(F32)

        blocks(sums[unit].shape[0], widen)

    for moment in range(units + 2):
        if moment < units:
            gather_peers(moment)
        if 1 <= moment <= units:
            inward(moment - 1)
        if moment >= 2:
            outward(moment - 2)
    for unit in range(units):
        near_copy(unit, early[unit]).wait_send()
        for step in range(1, depth):
            far_copy(unit, step).wait_send()

        @pl.when(has_outer)
        def _():
            remote(sums[unit], inner_in[unit], out_send.at[unit], inner_recv.at[unit], outer).wait_send()


def reduce_grads(early, later):
    depth, chain = lax.axis_size("fsdp"), lax.axis_size("replica")
    shapes = [item.shape for item in early]
    owned = [(rows // depth, columns) for rows, columns in shapes]
    others = [(rows - rows // depth, columns) for rows, columns in shapes]
    groups = (shapes, shapes, others, owned, owned, owned)
    dma = pltpu.SemaphoreType.DMA
    return pl.pallas_call(
        functools.partial(reduce_body, depth, chain),
        out_shape=[jax.ShapeDtypeStruct(shape, F32) for shape in owned],
        in_specs=[pl.BlockSpec(memory_space=pltpu.VMEM)] * 8,
        out_specs=[pl.BlockSpec(memory_space=pltpu.VMEM)] * 4,
        scratch_shapes=[pltpu.VMEM(shape, BF16) for group in groups for shape in group]
        + [dma((4,)), dma((4,)), dma((4, depth - 1)), dma((4, depth - 1)), dma((4,)), dma((4,)), dma((4,)), dma((4,))],
        compiler_params=pltpu.CompilerParams(collective_id=2, has_side_effects=True, vmem_limit_bytes=VMEM),
    )(*early, *later)


def pick(first, early, later):
    return jnp.where(first, early, later)


def on_device(
    images, cotangent, ln1_gain, ln1_bias, qkv_weight, qkv_bias, proj_weight, proj_bias, ln2_gain, ln2_bias,
    fc1_weight, fc1_bias, fc2_weight, fc2_bias, rel_table, rel_index, region,
):
    section = lax.axis_index("section")
    first = section == 0
    halves = lax.axis_size("section")
    count = images.shape[0] // halves
    every = ("section", "fsdp", "replica")
    swap = [(0, 1), (1, 0)]

    small = (ln1_gain, ln1_bias, qkv_bias, proj_bias, ln2_gain, ln2_bias, fc1_bias, fc2_bias, rel_table)
    sizes = [item[0].size for item in small]
    flat = jnp.concatenate([item.reshape(1, -1) for item in small], 1)
    both = lax.all_gather(flat, "section", axis=0, tiled=True)
    params = []
    for layer in range(2):
        pieces, start = [], 0
        for size in sizes:
            pieces.append(both[layer : layer + 1, start : start + size])
            start += size
        params.append(pieces)

    w_qkv, w_proj, w_fc1, w_fc2 = fetch([item[0] for item in (qkv_weight, proj_weight, fc1_weight, fc2_weight)])

    mine_x = lax.dynamic_slice_in_dim(images, section * count, count, 0)
    mine_g = lax.dynamic_slice_in_dim(cotangent, section * count, count, 0)

    edge = PAD - SPOTS
    index = jnp.pad(rel_index, ((0, edge), (0, edge)), constant_values=-1)
    onehot = (index.reshape(-1, 1) == jnp.arange(REL, dtype=jnp.int32)[None, :]).astype(F32)
    tables = jnp.concatenate([params[layer][8].reshape(REL, HEADS) for layer in range(2)], 1)
    spots = jnp.dot(onehot, tables, precision=lax.Precision.HIGHEST)
    spots = spots.reshape(PAD, PAD, 2, HEADS).transpose(2, 0, 3, 1)
    absent = jnp.where(jnp.arange(PAD) < SPOTS, 0.0, FAR).astype(F32)
    spots = spots + absent
    labels = region[np.maximum(window_tokens(0), 0)].reshape(WINDOWS, PAD)
    penalty = jnp.where(labels[:, :, None] != labels[:, None, :], -100.0, 0.0).astype(F32)
    biases = [
        spots[0].reshape(1, PAD, HEADS * PAD),
        (spots[1][None] + penalty[:, :, None, :]).reshape(WINDOWS, PAD, HEADS * PAD),
    ]

    places = [jnp.asarray(placement(shift), BF16) for shift in (0, SHIFT)]
    backs = [jnp.asarray(placement(shift).T, BF16) for shift in (0, SHIFT)]
    rows = count * ROWS
    dense = 2 * rows * D * D

    def forward(x, layer):
        gain_one, shift_one, b_qkv, b_proj, gain_two, shift_two, b_fc1, b_fc2, _ = params[layer]
        normed, packed, probs, attended, middle = run(
            attention_forward,
            (x, places[layer], w_qkv, w_proj, gain_one, shift_one, b_qkv, b_proj, biases[layer]),
            [((rows, D), BF16), ((rows, 3 * D), BF16), ((rows, HEADS * PAD), F32), ((rows, D), BF16), ((rows, D), F32)],
            layer, (2, 3), flops=12 * dense,
        )
        out, normed_two, activated, slope = run(
            feed_forward,
            (middle, backs[layer], w_fc1, w_fc2, gain_two, shift_two, b_fc1, b_fc2),
            [((count, TOKENS, D), BF16), ((rows, D), BF16), ((rows, FF), BF16), ((rows, FF), BF16)],
            layer, (2, 3), flops=12 * dense,
        )
        return out, (x, normed, packed, probs, attended, middle, normed_two, activated, slope)

    def backward(g, kept, layer):
        x, normed, packed, probs, attended, middle, normed_two, activated, slope = kept
        gain_one, gain_two = params[layer][0], params[layer][4]
        row = lambda width: ((1, width), F32)
        gfc1, gfc2, gmid, gbfc1, gbfc2, ggain2, gshift2 = run(
            feed_backward,
            (g, places[layer], normed_two, activated, slope, middle, w_fc1, w_fc2, gain_two),
            [((D, FF), BF16), ((FF, D), BF16), ((rows, D), F32), row(FF), row(D), row(D), row(D)],
            layer, (6, 7),
            (pltpu.VMEM((rows, D), BF16), pltpu.VMEM((rows, FF), BF16)), flops=20 * dense,
        )
        gqkv, gproj, gin, gbqkv, gbproj, ggain1, gshift1, gbias = run(
            attention_backward,
            (x, places[layer], backs[layer], gmid, probs, packed, attended, normed, w_qkv, w_proj, gain_one),
            [((D, 3 * D), BF16), ((D, D), BF16), ((count, TOKENS, D), BF16), row(3 * D), row(D), row(D), row(D),
             ((PAD, HEADS * PAD), F32)],
            layer, (8, 9),
            (pltpu.VMEM((rows, D), BF16), pltpu.VMEM((rows, D), BF16), pltpu.VMEM((rows, 3 * D), BF16)),
            flops=30 * dense,
        )
        gbias = gbias.reshape(PAD, HEADS, PAD).transpose(0, 2, 1).reshape(PAD * PAD, HEADS)
        gtable = jnp.dot(onehot.T, gbias, precision=lax.Precision.HIGHEST)
        minor = (ggain1, gshift1, gbqkv, gbproj, ggain2, gshift2, gbfc1, gbfc2, gtable.reshape(1, -1))
        minor = lax.psum(jnp.concatenate(minor, 1), every)
        return gin, (gfc2, gfc1, gqkv, gproj), minor

    def exchange(early, later):
        other = lax.ppermute(pick(first, later, early), "section", swap)
        own = pick(first, early, later)
        return jnp.concatenate([pick(first, own, other), pick(first, other, own)], 0)

    act_zero, kept_zero = forward(mine_x, 0)
    act_one, kept_one = forward(act_zero, 1)
    gin_one, grads_one, minor_one = backward(mine_g, kept_one, 1)
    gin_zero, grads_zero, minor_zero = backward(gin_one, kept_zero, 0)
    activations = exchange(act_zero, act_one)
    input_grad = exchange(gin_zero, gin_one)
    owned = reduce_grads(grads_zero, grads_one)
    owned = [owned[unit][None] for unit in (2, 3, 1, 0)]
    minor = pick(first, minor_zero, minor_one)
    minors, start = [], 0
    for size, item in zip(sizes, small):
        minors.append(minor[:, start : start + size].reshape(item.shape))
        start += size
    return (
        activations[None], input_grad[None],
        minors[0], minors[1], owned[0], minors[2], owned[1], minors[3], minors[4], minors[5],
        owned[2], minors[6], owned[3], minors[7], minors[8],
    )


def solution(mesh):
    sliced = P("section", "fsdp", None)
    vector = P("section", None)
    tokens = P(("fsdp", "replica"), None, None)
    in_specs = (
        tokens, tokens, vector, vector, sliced, vector, sliced, vector, vector, vector,
        sliced, vector, sliced, vector, P("section", None, None), P(), P(),
    )
    result = P("section", ("fsdp", "replica"), None, None)
    out_specs = (
        result, result, vector, vector, sliced, vector, sliced, vector, vector, vector,
        sliced, vector, sliced, vector, P("section", None, None),
    )
    return jax.shard_map(on_device, mesh=mesh, in_specs=in_specs, out_specs=out_specs, check_vma=False)
```
